32 devices in a mesh: node: 8 (over y, x, core), local: 4 (over z).
Axes of the slice: x: 2, y: 2, z: 4, core: 2. Of those that a mesh axis runs over, the one named last changes fastest.
Arguments:
- tokens: bfloat16 [4096, 5120], P('node', 'local'), may hold values from -6 to 6
- queries: bfloat16 [4096, 8192], P('node', 'local'), may hold values from -6 to 6
- key_weight: bfloat16 [5120, 1024], P('node', 'local'), may hold values from -0.078125 to 0.078125
- value_weight: bfloat16 [5120, 1024], P('node', 'local'), may hold values from -0.078125 to 0.078125
- query_gain: float32 [128], replicated, may hold values from 0.5 to 1.6
- key_gain: float32 [128], replicated, may hold values from 0.5 to 1.6
- segment_ids: int32 [8, 512], P('node'), may hold values from 0 to 255, never falling along the last dimension, each value on 1 to 256 neighbouring positions
- context_grad: bfloat16 [4096, 8192], P('node', 'local'), may hold values from -16 to 16
Outputs:
- context: bfloat16 [4096, 8192], P('node', 'local')
- token_grad: bfloat16 [4096, 5120], P('node', 'local')
- query_grad: bfloat16 [4096, 8192], P('node', 'local')
- key_weight_grad: float32 [5120, 1024], P('node', 'local')
- value_weight_grad: float32 [5120, 1024], P('node', 'local')
- gain_grads: float32 [2, 128], replicated
The draws below stay inside these ranges and needn't reach their ends.
Inputs may be any that keep to these rules, and one draw needn't show every extreme that they name: `segment_ids`: within each row the numbers never fall; a document is a run of equal numbers of at most half of 512 tokens.
All inputs are finite; a program needn't handle non-finite values.
Results may differ from the reference program's by a relative error of at most 0.014.
Values may be sent and summed in bfloat16 or wider, within the bound.
A program may use at most 128 MiB of HBM per device.

```python
import math
import jax
import jax.numpy as jnp
import numpy as np
from jax import lax

D = 5120
HEAD = 128
KV_HEADS = 8
Q_HEADS = 64
SEQ = 512
GROUP = 8
KV_DEV = 2
TOKENS = 4096
N_LOCAL = 4


def draw_context_grad(key, part):
    row_ramp = jnp.arange(TOKENS, dtype=jnp.float32) / TOKENS
    noise = jnp.clip(jax.random.normal(key, (TOKENS, Q_HEADS * HEAD), jnp.float32), -5.0, 5.0)
    row_scale = 1.0 + 2.0 * row_ramp
    return (noise * row_scale[:, None]).astype(jnp.bfloat16)


def steps_of(stream_key, shape, pieces, least, largest):
    level, own = 1.0, jax.random.fold_in(stream_key, 6)
    for dim, blocks in pieces:
        steps = jnp.exp(jax.random.uniform(jax.random.fold_in(own, dim), (blocks,), jnp.float32, least / len(pieces), largest / len(pieces)))
        level = level * jnp.repeat(steps, shape[dim] // blocks).reshape([-1 if axis == dim else 1 for axis in range(len(shape))])
    return level


def split_up(count, total, most, slope):
    portions = [(1 << 20) // math.isqrt(standing ** slope) + 1 for standing in range(2, count + 1)]
    rest, holding = total - most - (count - 1), [1] * (count - 1)
    while rest > 0:
        movable = [i for i in range(count - 1) if holding[i] < most]
        pool, left = sum([portions[i] for i in movable]), rest
        for i in movable:
            extra = min(most - holding[i], max(1, left * portions[i] // pool), rest)
            holding[i] = holding[i] + extra
            rest = rest - extra
    return np.array([most] + holding)


def ragged(own_key, amount, total, reach, slope):
    if amount == 2:
        one = jax.random.randint(own_key, (), max(1, total - reach), min(reach, total - 1) + 1)
        return jnp.stack([one, total - one])
    sizes = jnp.asarray(split_up(amount, total, reach, slope), jnp.int32)
    twos = (amount - 1) // 2
    source_of, receiver = sizes[1:1 + 2 * twos:2], sizes[2:2 + 2 * twos:2]
    margin = jnp.minimum(source_of - 1, reach - receiver)
    passed = jax.random.randint(jax.random.fold_in(own_key, 1), (twos,), 0, 1 << 20) % (margin + 1)
    sizes = sizes.at[1:1 + 2 * twos:2].set(source_of - passed).at[2:2 + 2 * twos:2].set(receiver + passed)
    return sizes[jax.random.permutation(jax.random.fold_in(own_key, 2), amount)]


def bell_draw(stream_key, extent, deviation, reach, split=(), held_as=jnp.bfloat16):
    values = jax.random.normal(stream_key, extent, jnp.float32) * deviation
    if len(split) > 0:
        values = steps_of(stream_key, extent, split, -0.22, 0.18) * values
    return jnp.clip(values, min=-reach, max=reach).astype(held_as)


def setup_inputs(seed: int = 0) -> dict:
    splits = jax.random.split(jax.random.key(seed), 9)
    return {
        "tokens": bell_draw(splits[0], (TOKENS, D), 1.0, 6.0, ((0, 8), (1, 4))),
        "queries": bell_draw(splits[1], (TOKENS, Q_HEADS * HEAD), 1.0, 6.0, ((0, 8), (1, 4))),
        "key_weight": bell_draw(splits[2], (D, KV_HEADS * HEAD), D ** -0.5, 0.078125, ((0, 8), (1, 4))),
        "value_weight": bell_draw(splits[3], (D, KV_HEADS * HEAD), D ** -0.5, 0.078125, ((0, 8), (1, 4))),
        "query_gain": jnp.clip(jnp.exp(jax.random.uniform(splits[4], (HEAD,), jnp.float32, math.log(0.5), math.log(1.6))), 0.5, 1.6),
        "key_gain": jnp.clip(jnp.exp(jax.random.uniform(splits[5], (HEAD,), jnp.float32, math.log(0.5), math.log(1.6))), 0.5, 1.6),
        "segment_ids": jax.vmap(lambda own: jnp.searchsorted(jnp.cumsum(ragged(own, SEQ // 2, SEQ, SEQ // 2, 2)), jnp.arange(SEQ), side="right"))(jax.random.split(splits[6], (TOKENS // SEQ))).reshape((TOKENS // SEQ, SEQ)).astype(jnp.int32),
        "context_grad": draw_context_grad(jax.random.fold_in(splits[8], 71), 0),
    }


EPS = 1e-06
THETA = 1000000.0

def rope_tables(segments, head_size):
    length = segments.shape[0]
    token_index = jnp.arange(length, dtype=jnp.int32)
    starts = jnp.concatenate([jnp.ones((1,), dtype=bool), segments[1:] != segments[:-1]])
    run_first = lax.cummax(jnp.where(starts, token_index, 0).astype(jnp.int32), axis=0)
    position = (token_index - run_first).astype(jnp.float32)
    frequency = THETA ** (-2.0 * jnp.arange(head_size // 2, dtype=jnp.float32) / head_size)
    angles = position[:, None] * frequency[None, :]
    return (jnp.cos(angles), jnp.sin(angles))

def rotate(values, cosine_table, sine_table):
    half_size = values.shape[-1] // 2
    first_half = values[..., :half_size]
    second_half = values[..., half_size:]
    cos_wide = cosine_table[:, None, :]
    sin_wide = sine_table[:, None, :]
    return jnp.concatenate([first_half * cos_wide - second_half * sin_wide, second_half * cos_wide + first_half * sin_wide], axis=-1)

def rotate_back(values, cosine_table, sine_table):
    half_size = values.shape[-1] // 2
    first_half = values[..., :half_size]
    second_half = values[..., half_size:]
    cos_wide = cosine_table[:, None, :]
    sin_wide = sine_table[:, None, :]
    return jnp.concatenate([first_half * cos_wide + second_half * sin_wide, second_half * cos_wide - first_half * sin_wide], axis=-1)

def normalize(values, gain_vector):
    inverse_rms = lax.rsqrt(lax.optimization_barrier(jnp.mean(values * values, axis=-1, keepdims=True)) + EPS)
    return (values * inverse_rms * gain_vector, inverse_rms)

def normalize_back(values, inverse_rms, gain_vector, upstream):
    weighted = gain_vector * upstream
    return inverse_rms * weighted - values * inverse_rms ** 3 * lax.optimization_barrier(jnp.mean(values * weighted, axis=-1, keepdims=True))

def sequence_pass(token_seq, query_seq, grad_seq, segments, key_weight, value_weight, query_gain, key_gain):
    seq_len = token_seq.shape[0]
    score_scale = HEAD ** (-0.5)
    cosine_table, sine_table = rope_tables(segments, HEAD)
    key_raw = jnp.dot(token_seq, key_weight, preferred_element_type=jnp.float32).reshape(seq_len, KV_HEADS, HEAD)
    value_bf = jnp.dot(token_seq, value_weight, preferred_element_type=jnp.float32).astype(jnp.bfloat16).reshape(seq_len, KV_HEADS, HEAD)
    key_normed, key_scale = normalize(key_raw, key_gain)
    key_rot = rotate(key_normed, cosine_table, sine_table).astype(jnp.bfloat16)
    query_wide = query_seq.astype(jnp.float32).reshape(seq_len, Q_HEADS, HEAD)
    query_normed, query_scale = normalize(query_wide, query_gain)
    query_rot = rotate(query_normed, cosine_table, sine_table).astype(jnp.bfloat16).reshape(seq_len, KV_HEADS, GROUP, HEAD)
    grad_rows = grad_seq.reshape(seq_len, KV_HEADS, GROUP, HEAD)
    token_index = jnp.arange(seq_len, dtype=jnp.int32)
    allowed = (segments[:, None] == segments[None, :]) & (token_index[None, :] <= token_index[:, None])

    def per_head(operands):
        query_head, key_head, value_head, grad_head = operands
        query_f = query_head.astype(jnp.float32)
        key_f = key_head.astype(jnp.float32)
        value_f = value_head.astype(jnp.float32)
        grad_f = grad_head.astype(jnp.float32)
        scores = jnp.einsum('qgh,kh->gqk', query_f, key_f) * score_scale
        exponent = jnp.where(allowed[None], jnp.exp(scores), 0.0)
        weights = exponent / lax.optimization_barrier(jnp.sum(exponent, axis=-1, keepdims=True))
        rounded = weights.astype(jnp.bfloat16).astype(jnp.float32)
        context_head = jnp.einsum('gqk,kh->qgh', rounded, value_f).astype(jnp.bfloat16)
        dot_grad = jnp.einsum('qgh,kh->gqk', grad_f, value_f)
        delta_row = lax.optimization_barrier(jnp.sum(weights * dot_grad, axis=-1, keepdims=True))
        score_grad = (weights * (dot_grad - delta_row) * score_scale).astype(jnp.bfloat16).astype(jnp.float32)
        value_grad = jnp.einsum('gqk,qgh->kh', rounded, grad_f).astype(jnp.bfloat16)
        query_rot_grad = jnp.einsum('gqk,kh->qgh', score_grad, key_f)
        key_rot_grad = jnp.einsum('gqk,qgh->kh', score_grad, query_f)
        return (context_head, value_grad, query_rot_grad, key_rot_grad)
    results = lax.map(per_head, (jnp.moveaxis(query_rot, 1, 0), jnp.moveaxis(key_rot, 1, 0), jnp.moveaxis(value_bf, 1, 0), jnp.moveaxis(grad_rows, 1, 0)))
    context = jnp.moveaxis(results[0], 0, 1).reshape(seq_len, Q_HEADS * HEAD)
    value_grad = jnp.moveaxis(results[1], 0, 1).reshape(seq_len, KV_HEADS * HEAD)
    query_rot_grad = jnp.moveaxis(results[2], 0, 1).reshape(seq_len, Q_HEADS, HEAD)
    key_rot_grad = jnp.moveaxis(results[3], 0, 1)
    query_normed_grad = rotate_back(query_rot_grad, cosine_table, sine_table)
    key_normed_grad = rotate_back(key_rot_grad, cosine_table, sine_table)
    query_grad = normalize_back(query_wide, query_scale, query_gain, query_normed_grad).astype(jnp.bfloat16).reshape(seq_len, Q_HEADS * HEAD)
    key_grad = normalize_back(key_raw, key_scale, key_gain, key_normed_grad).astype(jnp.bfloat16).reshape(seq_len, KV_HEADS * HEAD)
    gain_query = lax.optimization_barrier(jnp.sum(query_normed_grad * query_wide * query_scale, axis=(0, 1)))
    gain_key = lax.optimization_barrier(jnp.sum(key_normed_grad * key_raw * key_scale, axis=(0, 1)))
    key_part = jnp.dot(token_seq.T, key_grad, preferred_element_type=jnp.float32)
    value_part = jnp.dot(token_seq.T, value_grad, preferred_element_type=jnp.float32)
    block_width = KV_DEV * HEAD
    key_grad_blocks = key_grad.reshape(seq_len, N_LOCAL, block_width).astype(jnp.float32)
    value_grad_blocks = value_grad.reshape(seq_len, N_LOCAL, block_width).astype(jnp.float32)
    key_blocks = key_weight.reshape(D, N_LOCAL, block_width).astype(jnp.float32)
    value_blocks = value_weight.reshape(D, N_LOCAL, block_width).astype(jnp.float32)
    partial_value = jnp.einsum('snc,dnc->nsd', key_grad_blocks, key_blocks) + jnp.einsum('snc,dnc->nsd', value_grad_blocks, value_blocks)
    partial_bf = lax.optimization_barrier(partial_value.astype(jnp.bfloat16))
    token_grad = lax.optimization_barrier(jnp.sum(partial_bf.astype(jnp.float32), axis=0)).astype(jnp.bfloat16)
    return (context, token_grad, query_grad, key_part, value_part, jnp.stack([gain_query, gain_key]))

def reference(tokens, queries, key_weight, value_weight, query_gain, key_gain, segment_ids, context_grad):
    count_seq = segment_ids.shape[0]
    seq_len = segment_ids.shape[1]

    def step(totals, operands):
        token_seq, query_seq, grad_seq, segments = operands
        results = sequence_pass(token_seq, query_seq, grad_seq, segments, key_weight, value_weight, query_gain, key_gain)
        updated = (totals[0] + results[3], totals[1] + results[4], totals[2] + results[5])
        return (updated, (results[0], results[1], results[2]))
    initial = (jnp.zeros(key_weight.shape, jnp.float32), jnp.zeros(value_weight.shape, jnp.float32), jnp.zeros((2, HEAD), jnp.float32))
    operands = (tokens.reshape(count_seq, seq_len, D), queries.reshape(count_seq, seq_len, Q_HEADS * HEAD), context_grad.reshape(count_seq, seq_len, Q_HEADS * HEAD), segment_ids)
    totals, stacked = lax.scan(step, initial, operands)
    context = stacked[0].reshape(TOKENS, Q_HEADS * HEAD)
    token_grad = stacked[1].reshape(TOKENS, D)
    query_grad = stacked[2].reshape(TOKENS, Q_HEADS * HEAD)
    return (context, token_grad, query_grad, totals[0], totals[1], totals[2])
```

```python
import functools
import math

import jax
import jax.numpy as jnp
from jax import lax
from jax.experimental import pallas as pl
from jax.experimental.pallas import tpu as pltpu
from jax.sharding import PartitionSpec as P

EPS = 1e-06
THETA = 1000000.0
BLOCKED = -1e30


def tables(segments, head_size):
    length = segments.shape[0]
    token_index = jnp.arange(length, dtype=jnp.int32)
    starts = jnp.concatenate([jnp.ones((1,), dtype=bool), segments[1:] != segments[:-1]])
    run_first = lax.cummax(jnp.where(starts, token_index, 0), axis=0)
    position = (token_index - run_first).astype(jnp.float32)
    frequency = THETA ** (-2.0 * jnp.arange(head_size // 2, dtype=jnp.float32) / head_size)
    angles = frequency[:, None] * position[None, :]
    allowed = (segments[:, None] == segments[None, :]) & (
        token_index[:, None] <= token_index[None, :]
    )
    bias = jnp.where(allowed, 0.0, BLOCKED).astype(jnp.float32)
    return jnp.cos(angles), jnp.sin(angles), bias


def turn(values, c1, s1, c2, s2):
    half = values.shape[0] // 2
    a, b = values[:half], values[half:]
    return jnp.concatenate([a * c1 - b * s2, b * c2 + a * s1], axis=0)


def turn_back(values, c1, s1, c2, s2):
    half = values.shape[0] // 2
    a, b = values[:half], values[half:]
    return jnp.concatenate([a * c1 + b * s1, b * c2 - a * s2], axis=0)


def attention_kernel(
    heads, block, window,
    q_ref, g_ref, k_ref, v_ref, cos_ref, sin_ref, bias_ref, gain_ref,
    ctx_ref, qg_ref, kg_ref, vg_ref, gains_ref,
    qtab, kt, kn, vt, vn, dk, dv, gq, gk,
):
    c, g = pl.program_id(0), pl.program_id(1)
    last_c, last_g = pl.num_programs(0) - 1, pl.num_programs(1) - 1
    seq, head = k_ref.shape
    half = head // 2
    score_scale = head ** (-0.5)
    exp_scale = score_scale * math.log2(math.e)

    @pl.when((c == 0) & (g == 0))
    def _():
        gq[...] = jnp.zeros_like(gq)
        gk[...] = jnp.zeros_like(gk)
        cos, sin = cos_ref[...], sin_ref[...]
        for which in range(2):
            low = gain_ref[:half, which : which + 1]
            high = gain_ref[half:, which : which + 1]
            qtab[4 * which + 0] = low * cos
            qtab[4 * which + 1] = low * sin
            qtab[4 * which + 2] = high * cos
            qtab[4 * which + 3] = high * sin

    @pl.when(g == 0)
    def _():
        raw = k_ref[...].T
        scale = lax.rsqrt(jnp.mean(raw * raw, axis=0, keepdims=True) + EPS)
        rot = turn(raw, qtab[4], qtab[5], qtab[6], qtab[7]) * scale
        kt[...] = rot.astype(jnp.bfloat16)
        kn[...] = rot.T.astype(jnp.bfloat16)
        values = v_ref[...]
        vn[...] = values.astype(jnp.bfloat16)
        vt[...] = values.T.astype(jnp.bfloat16)
        dk[...] = jnp.zeros_like(dk)
        dv[...] = jnp.zeros_like(dv)

    c1, s1, c2, s2 = qtab[0], qtab[1], qtab[2], qtab[3]
    for h in range(heads):
        cols = slice(h * head, (h + 1) * head)
        q = q_ref[:, cols].astype(jnp.float32).T
        grad = g_ref[:, cols]
        grad_t = grad.astype(jnp.float32).T.astype(jnp.bfloat16)
        scale = lax.rsqrt(jnp.mean(q * q, axis=0, keepdims=True) + EPS)
        rot = turn(q, c1, s1, c2, s2) * scale
        rot_t = rot.astype(jnp.bfloat16)
        rot_n = rot.T.astype(jnp.bfloat16)
        parts = []
        for start in range(0, seq, block):
            stop = start + block
            first = max(0, (start - window + 1) // block * block)
            keys = slice(first, stop)
            rows = slice(start, stop)
            s = jnp.dot(kn[keys], rot_t[:, rows], preferred_element_type=jnp.float32)
            e = jnp.exp2(s * exp_scale + bias_ref[keys, rows])
            inv = 1.0 / jnp.sum(e, axis=0, keepdims=True)
            w = e * inv
            p = w.astype(jnp.bfloat16)
            dp = jnp.dot(vn[keys], grad_t[:, rows], preferred_element_type=jnp.float32)
            delta = jnp.sum(w * dp, axis=0, keepdims=True)
            ds = (w * (dp - delta)).astype(jnp.bfloat16)
            ctx = jnp.dot(vt[:, keys], p, preferred_element_type=jnp.float32)
            ctx_ref[rows, cols] = ctx.T.astype(jnp.bfloat16)
            parts.append(jnp.dot(kt[:, keys], ds, preferred_element_type=jnp.float32))
            dv[keys] += jnp.dot(p, grad[rows], preferred_element_type=jnp.float32)
            dk[keys] += jnp.dot(ds, rot_n[rows], preferred_element_type=jnp.float32)
        rot_grad = jnp.concatenate(parts, axis=1)
        u = turn_back(rot_grad, c1, s1, c2, s2)
        scale_u = scale * score_scale
        t = q * u
        mean = jnp.mean(t, axis=0, keepdims=True)
        gq[...] += t * scale_u
        q_grad = u * scale_u - q * (scale * scale * scale_u * mean)
        qg_ref[:, cols] = q_grad.T.astype(jnp.bfloat16)

    @pl.when(g == last_g)
    def _():
        raw = k_ref[...].T
        scale = lax.rsqrt(jnp.mean(raw * raw, axis=0, keepdims=True) + EPS)
        u = turn_back(dk[...].T, qtab[4], qtab[5], qtab[6], qtab[7])
        scale_u = scale * score_scale
        t = raw * u
        mean = jnp.mean(t, axis=0, keepdims=True)
        gk[...] += t * scale_u
        k_grad = u * scale_u - raw * (scale * scale * scale_u * mean)
        kg_ref[...] = k_grad.T.astype(jnp.bfloat16)
        vg_ref[...] = dv[...].astype(jnp.bfloat16)

    @pl.when((c == last_c) & (g == last_g))
    def _():
        gains_ref[0:1] = (jnp.sum(gq[...], axis=1, keepdims=True) / gain_ref[:, 0:1]).T
        gains_ref[1:2] = (jnp.sum(gk[...], axis=1, keepdims=True) / gain_ref[:, 1:2]).T


def attention(queries, context_grad, projected, cos, sin, bias, gains, head, block=256, heads=4):
    seq, width = queries.shape
    kv = projected.shape[1] // (2 * head)
    group = width // head // kv
    heads = math.gcd(heads, group)
    steps = group // heads
    wide = pl.BlockSpec((seq, heads * head), lambda c, g: (0, c * steps + g))
    narrow = pl.BlockSpec((seq, head), lambda c, g: (0, c))
    whole = lambda shape: pl.BlockSpec(shape, lambda c, g: (0, 0))
    f32, bf16 = jnp.float32, jnp.bfloat16
    return pl.pallas_call(
        functools.partial(attention_kernel, heads, block, seq // 2),
        grid=(kv, steps),
        in_specs=[
            wide,
            wide,
            narrow,
            pl.BlockSpec((seq, head), lambda c, g: (0, kv + c)),
            whole(cos.shape),
            whole(sin.shape),
            whole(bias.shape),
            whole(gains.shape),
        ],
        out_specs=[wide, wide, narrow, narrow, whole((2, head))],
        out_shape=[
            jax.ShapeDtypeStruct((seq, width), bf16),
            jax.ShapeDtypeStruct((seq, width), bf16),
            jax.ShapeDtypeStruct((seq, kv * head), bf16),
            jax.ShapeDtypeStruct((seq, kv * head), bf16),
            jax.ShapeDtypeStruct((2, head), f32),
        ],
        scratch_shapes=[
            pltpu.VMEM((8, head // 2, seq), f32),
            pltpu.VMEM((head, seq), bf16),
            pltpu.VMEM((seq, head), bf16),
            pltpu.VMEM((head, seq), bf16),
            pltpu.VMEM((seq, head), bf16),
            pltpu.VMEM((seq, head), f32),
            pltpu.VMEM((seq, head), f32),
            pltpu.VMEM((head, seq), f32),
            pltpu.VMEM((head, seq), f32),
        ],
        compiler_params=pltpu.CompilerParams(
            dimension_semantics=("arbitrary", "arbitrary"), vmem_limit_bytes=48 * 2**20
        ),
        cost_estimate=pl.CostEstimate(
            flops=9 * seq * seq * width, bytes_accessed=8 * seq * width, transcendentals=0
        ),
    )(queries, context_grad, projected, projected, cos, sin, bias, gains)


def local(
    tokens, queries, key_weight, value_weight, query_gain, key_gain, segment_ids, context_grad
):
    head = query_gain.shape[0]
    kv_width = key_weight.shape[1]
    cos, sin, bias = tables(segment_ids[0], head)
    gains = jnp.stack([query_gain, key_gain], axis=1)
    gathered = lax.all_gather(tokens, "local", axis=1, tiled=True)
    stacked = jnp.concatenate([key_weight, value_weight], axis=1)
    weight_all = lax.all_gather(stacked, "node", axis=0, tiled=True)
    projected = jnp.dot(gathered, weight_all, preferred_element_type=jnp.float32)
    context, query_grad, key_grad, value_grad, gain_part = attention(
        queries, context_grad, projected, cos, sin, bias, gains, head
    )
    grad_stack = jnp.concatenate([key_grad, value_grad], axis=1)
    summed = lax.psum_scatter(
        lax.dot_general(
            weight_all, grad_stack, (((1,), (1,)), ((), ())), preferred_element_type=jnp.float32
        ).astype(jnp.bfloat16),
        "local",
        scatter_dimension=0,
        tiled=True,
    )
    token_grad = summed.T
    weight_grad = lax.psum_scatter(
        lax.dot_general(
            gathered, grad_stack, (((0,), (0,)), ((), ())), preferred_element_type=jnp.float32
        ).astype(jnp.bfloat16),
        "node",
        scatter_dimension=0,
        tiled=True,
    ).astype(jnp.float32)
    gain_grads = lax.psum(gain_part, ("node", "local"))
    key_weight_grad = weight_grad[:, :kv_width]
    value_weight_grad = weight_grad[:, kv_width:]
    return (context, token_grad, query_grad, key_weight_grad, value_weight_grad, gain_grads)


def solution(mesh):
    spread = P("node", "local")
    in_specs = (spread, spread, spread, spread, P(), P(), P("node", None), spread)
    out_specs = (spread, spread, spread, spread, spread, P())
    return jax.shard_map(local, mesh=mesh, in_specs=in_specs, out_specs=out_specs, check_vma=False)
```

```python
import functools
import math

import jax
import jax.numpy as jnp
from jax import lax
from jax.experimental import pallas as pl
from jax.experimental.pallas import tpu as pltpu
from jax.sharding import PartitionSpec as P

EPS = 1e-06
THETA = 1000000.0
BLOCKED = -1e30


def tables(segments, head_size):
    length = segments.shape[0]
    token_index = jnp.arange(length, dtype=jnp.int32)
    starts = jnp.concatenate([jnp.ones((1,), dtype=bool), segments[1:] != segments[:-1]])
    run_first = lax.cummax(jnp.where(starts, token_index, 0), axis=0)
    position = (token_index - run_first).astype(jnp.float32)
    frequency = THETA ** (-2.0 * jnp.arange(head_size // 2, dtype=jnp.float32) / head_size)
    angles = frequency[:, None] * position[None, :]
    allowed = (segments[:, None] == segments[None, :]) & (
        token_index[:, None] <= token_index[None, :]
    )
    bias = jnp.where(allowed, 0.0, BLOCKED).astype(jnp.float32)
    return jnp.cos(angles), jnp.sin(angles), bias


def turn(values, c1, s1, c2, s2):
    half = values.shape[0] // 2
    a, b = values[:half], values[half:]
    return jnp.concatenate([a * c1 - b * s2, b * c2 + a * s1], axis=0)


def turn_back(values, c1, s1, c2, s2):
    half = values.shape[0] // 2
    a, b = values[:half], values[half:]
    return jnp.concatenate([a * c1 + b * s1, b * c2 - a * s2], axis=0)


def attention_kernel(
    heads, block, window,
    q_ref, g_ref, k_ref, v_ref, cos_ref, sin_ref, bias_ref, gain_ref,
    ctx_ref, qg_ref, kg_ref, vg_ref, gains_ref,
    qtab, kt, kn, vt, vn, dk, dv, gq, gk,
):
    c, g = pl.program_id(0), pl.program_id(1)
    last_c, last_g = pl.num_programs(0) - 1, pl.num_programs(1) - 1
    seq, head = k_ref.shape
    half = head // 2
    score_scale = head ** (-0.5)
    exp_scale = score_scale * math.log2(math.e)

    @pl.when((c == 0) & (g == 0))
    def _():
        gq[...] = jnp.zeros_like(gq)
        gk[...] = jnp.zeros_like(gk)
        cos, sin = cos_ref[...], sin_ref[...]
        for which in range(2):
            low = gain_ref[:half, which : which + 1]
            high = gain_ref[half:, which : which + 1]
            qtab[4 * which + 0] = low * cos
            qtab[4 * which + 1] = low * sin
            qtab[4 * which + 2] = high * cos
            qtab[4 * which + 3] = high * sin

    @pl.when(g == 0)
    def _():
        raw = k_ref[...].T
        scale = lax.rsqrt(jnp.mean(raw * raw, axis=0, keepdims=True) + EPS)
        rot = turn(raw, qtab[4], qtab[5], qtab[6], qtab[7]) * scale
        kt[...] = rot.astype(jnp.bfloat16)
        kn[...] = rot.T.astype(jnp.bfloat16)
        values = v_ref[...]
        vn[...] = values.astype(jnp.bfloat16)
        vt[...] = values.T.astype(jnp.bfloat16)
        dk[...] = jnp.zeros_like(dk)
        dv[...] = jnp.zeros_like(dv)

    c1, s1, c2, s2 = qtab[0], qtab[1], qtab[2], qtab[3]
    for h in range(heads):
        cols = slice(h * head, (h + 1) * head)
        q = q_ref[:, cols].astype(jnp.float32).T
        grad = g_ref[:, cols]
        grad_t = grad.astype(jnp.float32).T.astype(jnp.bfloat16)
        scale = lax.rsqrt(jnp.mean(q * q, axis=0, keepdims=True) + EPS)
        rot = turn(q, c1, s1, c2, s2) * scale
        rot_t = rot.astype(jnp.bfloat16)
        rot_n = rot.T.astype(jnp.bfloat16)
        parts = []
        for start in range(0, seq, block):
            stop = start + block
            first = max(0, (start - window + 1) // block * block)
            keys = slice(first, stop)
            rows = slice(start, stop)
            s = jnp.dot(kn[keys], rot_t[:, rows], preferred_element_type=jnp.float32)
            e = jnp.exp2(s * exp_scale + bias_ref[keys, rows])
            inv = 1.0 / jnp.sum(e, axis=0, keepdims=True)
            w = e * inv
            p = w.astype(jnp.bfloat16)
            dp = jnp.dot(vn[keys], grad_t[:, rows], preferred_element_type=jnp.float32)
            delta = jnp.sum(w * dp, axis=0, keepdims=True)
            ds = (w * (dp - delta)).astype(jnp.bfloat16)
            ctx = jnp.dot(vt[:, keys], p, preferred_element_type=jnp.float32)
            ctx_ref[rows, cols] = ctx.T.astype(jnp.bfloat16)
            parts.append(jnp.dot(kt[:, keys], ds, preferred_element_type=jnp.float32))
            dv[keys] += jnp.dot(p, grad[rows], preferred_element_type=jnp.float32)
            dk[keys] += jnp.dot(ds, rot_n[rows], preferred_element_type=jnp.float32)
        rot_grad = jnp.concatenate(parts, axis=1)
        u = turn_back(rot_grad, c1, s1, c2, s2)
        scale_u = scale * score_scale
        t = q * u
        mean = jnp.mean(t, axis=0, keepdims=True)
        gq[...] += t * scale_u
        q_grad = u * scale_u - q * (scale * scale * scale_u * mean)
        qg_ref[:, cols] = q_grad.T.astype(jnp.bfloat16)

    @pl.when(g == last_g)
    def _():
        raw = k_ref[...].T
        scale = lax.rsqrt(jnp.mean(raw * raw, axis=0, keepdims=True) + EPS)
        u = turn_back(dk[...].T, qtab[4], qtab[5], qtab[6], qtab[7])
        scale_u = scale * score_scale
        t = raw * u
        mean = jnp.mean(t, axis=0, keepdims=True)
        gk[...] += t * scale_u
        k_grad = u * scale_u - raw * (scale * scale * scale_u * mean)
        kg_ref[...] = k_grad.T.astype(jnp.bfloat16)
        vg_ref[...] = dv[...].astype(jnp.bfloat16)

    @pl.when((c == last_c) & (g == last_g))
    def _():
        gains_ref[0:1] = (jnp.sum(gq[...], axis=1, keepdims=True) / gain_ref[:, 0:1]).T
        gains_ref[1:2] = (jnp.sum(gk[...], axis=1, keepdims=True) / gain_ref[:, 1:2]).T


def attention(queries, context_grad, projected, cos, sin, bias, gains, head, block=256, heads=4):
    seq, width = queries.shape
    kv = projected.shape[1] // (2 * head)
    group = width // head // kv
    heads = math.gcd(heads, group)
    steps = group // heads
    wide = pl.BlockSpec((seq, heads * head), lambda c, g: (0, c * steps + g))
    narrow = pl.BlockSpec((seq, head), lambda c, g: (0, c))
    whole = lambda shape: pl.BlockSpec(shape, lambda c, g: (0, 0))
    f32, bf16 = jnp.float32, jnp.bfloat16
    return pl.pallas_call(
        functools.partial(attention_kernel, heads, block, seq // 2),
        grid=(kv, steps),
        in_specs=[
            wide,
            wide,
            narrow,
            pl.BlockSpec((seq, head), lambda c, g: (0, kv + c)),
            whole(cos.shape),
            whole(sin.shape),
            whole(bias.shape),
            whole(gains.shape),
        ],
        out_specs=[wide, wide, narrow, narrow, whole((2, head))],
        out_shape=[
            jax.ShapeDtypeStruct((seq, width), bf16),
            jax.ShapeDtypeStruct((seq, width), bf16),
            jax.ShapeDtypeStruct((seq, kv * head), bf16),
            jax.ShapeDtypeStruct((seq, kv * head), bf16),
            jax.ShapeDtypeStruct((2, head), f32),
        ],
        scratch_shapes=[
            pltpu.VMEM((8, head // 2, seq), f32),
            pltpu.VMEM((head, seq), bf16),
            pltpu.VMEM((seq, head), bf16),
            pltpu.VMEM((head, seq), bf16),
            pltpu.VMEM((seq, head), bf16),
            pltpu.VMEM((seq, head), f32),
            pltpu.VMEM((seq, head), f32),
            pltpu.VMEM((head, seq), f32),
            pltpu.VMEM((head, seq), f32),
        ],
        compiler_params=pltpu.CompilerParams(
            dimension_semantics=("arbitrary", "arbitrary"), vmem_limit_bytes=48 * 2**20
        ),
        cost_estimate=pl.CostEstimate(
            flops=9 * seq * seq * width, bytes_accessed=8 * seq * width, transcendentals=0
        ),
    )(queries, context_grad, projected, projected, cos, sin, bias, gains)


def line_gather(size, me, own_ref, all_ref, send_sem, recv_sem):
    def copy(way, step, block, source):
        return pltpu.make_async_remote_copy(
            src_ref=source,
            dst_ref=all_ref.at[block],
            send_sem=send_sem.at[way, step],
            recv_sem=recv_sem.at[way, step],
            device_id={"local": me + 1 if way == 0 else me - 1},
            device_id_type=pl.DeviceIdType.MESH,
        )

    def sent(way, step):
        block = me - step if way == 0 else me + step
        return block, (block >= 0) & (me + 1 < size) if way == 0 else (block < size) & (me >= 1)

    def begin(way, step):
        block, there = sent(way, step)

        @pl.when(there)
        def _():
            copy(way, step, block, own_ref if step == 0 else all_ref.at[block]).start()

    def arrive(step):
        for way in range(2):
            block = me - 1 - step if way == 0 else me + 1 + step

            @pl.when(block >= 0 if way == 0 else block < size)
            def _():
                copy(way, step, block, own_ref).wait_recv()

            if step + 1 < size - 1:
                begin(way, step + 1)

    def finish():
        for step in range(size - 1):
            for way in range(2):
                block, there = sent(way, step)

                @pl.when(there)
                def _():
                    copy(way, step, block, own_ref).wait_send()

    def start():
        for way in range(2):
            begin(way, 0)

    return start, arrive, finish


def greet(nodes, locals_, node, me, all_locals, more=0):
    barrier = pltpu.get_barrier_semaphore()

    def signal(device):
        pl.semaphore_signal(
            barrier, inc=1, device_id=device, device_id_type=pl.DeviceIdType.MESH
        )

    for j in range(1, nodes):
        signal({"node": lax.rem(node + j, nodes)})
    if all_locals:
        for j in range(1, locals_):
            signal({"local": lax.rem(me + j, locals_)})
        pl.semaphore_wait(barrier, nodes - 1 + locals_ - 1)
    else:
        for edge, to in ((me >= 1, me - 1), (me + 1 < locals_, me + 1)):

            @pl.when(edge)
            def _():
                signal({"local": to})

        near = jnp.where(me >= 1, 1, 0) + jnp.where(me + 1 < locals_, 1, 0)
        pl.semaphore_wait(barrier, nodes - 1 + near + more)


def exchange(axis, size, me, slots, send_sem, recv_sem):
    def copy(j, slot):
        return pltpu.make_async_remote_copy(
            src_ref=slots.at[slot],
            dst_ref=slots.at[slot],
            send_sem=send_sem.at[j - 1],
            recv_sem=recv_sem.at[j - 1],
            device_id={axis: lax.rem(me + j, size)},
            device_id_type=pl.DeviceIdType.MESH,
        )

    def start():
        for j in range(1, size):
            copy(j, me).start()

    def finish():
        for j in range(1, size):
            copy(j, lax.rem(me + size - j, size)).wait_recv()
        for j in range(1, size):
            copy(j, me).wait_send()

    return start, finish


def pair_exchange(size, me, slots, same_send, same_recv, cross_send, cross_recv):
    half, parity, place = size // 2, lax.rem(me, 2), me // 2

    def slot(j, side):
        return lax.rem(place + half - j, half) * 2 + side

    def same(j, which):
        return pltpu.make_async_remote_copy(
            src_ref=slots.at[which],
            dst_ref=slots.at[which],
            send_sem=same_send.at[j],
            recv_sem=same_recv.at[j],
            device_id={"node": lax.rem(place + j, half) * 2 + parity},
            device_id_type=pl.DeviceIdType.MESH,
        )

    def cross(j, which):
        return pltpu.make_async_remote_copy(
            src_ref=slots.at[which],
            dst_ref=slots.at[which],
            send_sem=cross_send.at[j],
            recv_sem=cross_recv.at[j],
            device_id={"node": me + 1 - 2 * parity},
            device_id_type=pl.DeviceIdType.MESH,
        )

    def start():
        for j in range(1, half):
            same(j, me).start()
        cross(0, me).start()

    def relay():
        for j in range(1, half):
            same(j, slot(j, parity)).wait_recv()
            cross(j, slot(j, parity)).start()

    def arrived():
        for j in range(half):
            cross(j, slot(j, 1 - parity)).wait_recv()

    def finish():
        for j in range(1, half):
            same(j, me).wait_send()
        for j in range(half):
            cross(j, slot(j, parity)).wait_send()

    return start, relay, arrived, finish


def project_kernel(
    nodes, locals_, tokens_ref, kw_ref, vw_ref, all_ref, out_ref, rows_ref,
    slots, line_send, line_recv, col_sems, row_sems, trade_sems, own_sem,
):
    node, me = lax.axis_index("node"), lax.axis_index("local")
    ratio = nodes // locals_
    kv_width = kw_ref.shape[1]
    seq, depth = tokens_ref.shape
    rows = kw_ref.shape[0]
    own = pltpu.make_async_copy(tokens_ref, all_ref.at[me], own_sem)
    own.start()
    slots[node, :, :kv_width] = kw_ref[...]
    slots[node, :, kv_width:] = vw_ref[...]
    peer_node, peer_local = me * ratio + lax.rem(node, ratio), node // ratio
    moves = peer_local != me
    peer = {"node": peer_node, "local": peer_local}

    @pl.when(moves)
    def _():
        barrier = pltpu.get_barrier_semaphore()
        pl.semaphore_signal(
            barrier, inc=1, device_id=peer, device_id_type=pl.DeviceIdType.MESH
        )

    greet(nodes, locals_, node, me, False, jnp.where(moves, 1, 0))

    def trade(slot):
        return pltpu.make_async_remote_copy(
            src_ref=slots.at[node],
            dst_ref=rows_ref.at[slot],
            send_sem=trade_sems.at[0],
            recv_sem=trade_sems.at[1],
            device_id=peer,
            device_id_type=pl.DeviceIdType.MESH,
        )

    @pl.when(moves)
    def _():
        trade(peer_node).start()

    @pl.when(jnp.logical_not(moves))
    def _():
        rows_ref[node, :, :kv_width] = kw_ref[...]
        rows_ref[node, :, kv_width:] = vw_ref[...]

    start, arrive, finish = line_gather(
        locals_, me, tokens_ref, all_ref, line_send, line_recv
    )
    col_start, col_relay, col_arrived, col_finish = pair_exchange(
        nodes, node, slots, *(col_sems.at[i] for i in range(4))
    )
    row_start, row_relay, row_arrived, row_finish = pair_exchange(
        nodes, node, rows_ref, *(row_sems.at[i] for i in range(4))
    )
    start()
    col_start()
    out_ref[...] = jnp.zeros_like(out_ref)
    own.wait()

    def multiply(block):
        tile = min(256, seq)

        @pl.loop(0, seq // tile)
        def _(i):
            lines = pl.ds(pl.multiple_of(i * tile, tile), tile)
            total = out_ref[lines, :]
            for r in range(ratio):
                total += jnp.dot(
                    all_ref[block, lines, r * rows : (r + 1) * rows],
                    slots[block * ratio + r],
                    preferred_element_type=jnp.float32,
                )
            out_ref[lines, :] = total

    col_relay()
    if locals_ > 2:
        arrive(0)

    @pl.when(moves)
    def _():
        trade(node).wait_recv()

    row_start()
    for step in range(1, locals_ - 2):
        arrive(step)
    row_relay()
    col_arrived()

    @pl.loop(0, locals_)
    def _(block):
        @pl.when((block - me < locals_ - 1) & (me - block < locals_ - 1))
        def _():
            multiply(block)

    arrive(locals_ - 2)

    @pl.when((me == 0) | (me == locals_ - 1))
    def _():
        multiply(locals_ - 1 - me)

    row_arrived()
    finish()
    col_finish()
    row_finish()

    @pl.when(moves)
    def _():
        trade(peer_node).wait_send()


def project(nodes, locals_, tokens, key_weight, value_weight):
    seq, depth = tokens.shape
    rows, kv_width = key_weight.shape
    vmem = pl.BlockSpec(memory_space=pltpu.VMEM)
    return pl.pallas_call(
        functools.partial(project_kernel, nodes, locals_),
        in_specs=[vmem] * 3,
        out_specs=[vmem] * 3,
        out_shape=[
            jax.ShapeDtypeStruct((locals_, seq, depth), jnp.bfloat16),
            jax.ShapeDtypeStruct((seq, 2 * kv_width), jnp.float32),
            jax.ShapeDtypeStruct((nodes, rows, 2 * kv_width), jnp.bfloat16),
        ],
        scratch_shapes=[
            pltpu.VMEM((nodes, rows, 2 * kv_width), jnp.bfloat16),
            pltpu.SemaphoreType.DMA((2, locals_ - 1)),
            pltpu.SemaphoreType.DMA((2, locals_ - 1)),
            pltpu.SemaphoreType.DMA((4, nodes // 2)),
            pltpu.SemaphoreType.DMA((4, nodes // 2)),
            pltpu.SemaphoreType.DMA((2,)),
            pltpu.SemaphoreType.DMA,
        ],
        compiler_params=pltpu.CompilerParams(
            collective_id=0, has_side_effects=True, vmem_limit_bytes=40 * 2**20
        ),
        cost_estimate=pl.CostEstimate(
            flops=4 * seq * depth * locals_ * kv_width,
            bytes_accessed=200 * 2**20,
            transcendentals=0,
        ),
    )(tokens, key_weight, value_weight)


def gather_kernel(
    nodes, locals_, kg_ref, vg_ref, gain_ref, all_ref, sum_ref,
    near, far, line_send, line_recv, node_send, node_recv, local_send, local_recv,
):
    node, me = lax.axis_index("node"), lax.axis_index("local")
    kv_width = kg_ref.shape[1]
    all_ref[me, :, :kv_width] = kg_ref[...]
    all_ref[me, :, kv_width:] = vg_ref[...]
    near[node] = gain_ref[...]
    greet(nodes, locals_, node, me, True)
    start, arrive, finish = line_gather(
        locals_, me, all_ref.at[me], all_ref, line_send, line_recv
    )
    node_start, node_finish = exchange("node", nodes, node, near, node_send, node_recv)
    local_start, local_finish = exchange("local", locals_, me, far, local_send, local_recv)
    node_start()
    start()
    node_finish()
    far[me] = jnp.sum(near[...], axis=0)
    local_start()
    for step in range(locals_ - 1):
        arrive(step)
    local_finish()
    sum_ref[...] = jnp.sum(far[...], axis=0)
    finish()


def gather(nodes, locals_, key_grad, value_grad, gain_part):
    seq, kv_width = key_grad.shape
    vmem = pl.BlockSpec(memory_space=pltpu.VMEM)
    return pl.pallas_call(
        functools.partial(gather_kernel, nodes, locals_),
        in_specs=[vmem] * 3,
        out_specs=[vmem] * 2,
        out_shape=[
            jax.ShapeDtypeStruct((locals_, seq, 2 * kv_width), jnp.bfloat16),
            jax.ShapeDtypeStruct(gain_part.shape, jnp.float32),
        ],
        scratch_shapes=[
            pltpu.VMEM((nodes, *gain_part.shape), jnp.float32),
            pltpu.VMEM((locals_, *gain_part.shape), jnp.float32),
            pltpu.SemaphoreType.DMA((2, locals_ - 1)),
            pltpu.SemaphoreType.DMA((2, locals_ - 1)),
            pltpu.SemaphoreType.DMA((nodes - 1,)),
            pltpu.SemaphoreType.DMA((nodes - 1,)),
            pltpu.SemaphoreType.DMA((locals_ - 1,)),
            pltpu.SemaphoreType.DMA((locals_ - 1,)),
        ],
        compiler_params=pltpu.CompilerParams(
            collective_id=1, has_side_effects=True, vmem_limit_bytes=24 * 2**20
        ),
        cost_estimate=pl.CostEstimate(flops=0, bytes_accessed=100 * 2**20, transcendentals=0),
    )(key_grad, value_grad, gain_part)


def local(
    nodes, locals_, tokens, queries, key_weight, value_weight, query_gain, key_gain, segment_ids,
    context_grad,
):
    head = query_gain.shape[0]
    rows, kv_width = key_weight.shape
    ratio = nodes // locals_
    cos, sin, bias = tables(segment_ids[0], head)
    gains = jnp.stack([query_gain, key_gain], axis=1)
    gathered, projected, weight = project(nodes, locals_, tokens, key_weight, value_weight)
    weight = weight.reshape(locals_, ratio * rows, 2 * kv_width)
    context, query_grad, key_grad, value_grad, gain_part = attention(
        queries, context_grad, projected, cos, sin, bias, gains, head
    )
    grads = jnp.concatenate([key_grad, value_grad], axis=1)
    weight_part = jnp.einsum("lsf,sc->lfc", gathered, grads, preferred_element_type=jnp.float32)
    weight_part = weight_part.astype(jnp.bfloat16).reshape(nodes * rows, 2 * kv_width)
    weight_part, gain_part = lax.optimization_barrier((weight_part, gain_part))
    summed = lax.psum_scatter(weight_part, "node", scatter_dimension=0, tiled=True)
    grads_all, gain_grads = gather(nodes, locals_, key_grad, value_grad, gain_part)
    token_grad = jnp.einsum(
        "lsc,lfc->sf", grads_all, weight, preferred_element_type=jnp.float32
    ).astype(jnp.bfloat16)
    weight_grad = summed.astype(jnp.float32)
    key_weight_grad = weight_grad[:, :kv_width]
    value_weight_grad = weight_grad[:, kv_width:]
    return (context, token_grad, query_grad, key_weight_grad, value_weight_grad, gain_grads)


def solution(mesh):
    spread = P("node", "local")
    in_specs = (spread, spread, spread, spread, P(), P(), P("node", None), spread)
    out_specs = (spread, spread, spread, spread, spread, P())
    part = functools.partial(local, mesh.shape["node"], mesh.shape["local"])
    return jax.shard_map(part, mesh=mesh, in_specs=in_specs, out_specs=out_specs, check_vma=False)
```
